32 devices in a mesh: parts: 2 (over y), holder: 4 (over x, core), query: 4 (over z).
Axes of the slice: x: 2, y: 2, z: 4, core: 2. Of those that a mesh axis runs over, the one named last changes fastest.
Arguments:
- queries: bfloat16 [32, 32, 128], P(('parts', 'holder', 'query')), parts along dimension 0, may hold values from -6 to 6
- candidates: int32 [32, 256], P(('parts', 'holder', 'query')), parts along dimension 0, may hold values from 0 to 511, all different within a row; in each aligned block of 16 rows (0 to 15, 16 to 31, ...) at most 16 rows name the same one
- page_slot: int32 [1024], P('parts'), parts along dimension 0, may hold values from 0 to 511, each once
- page_embeddings: bfloat16 [1024, 1024, 128], P(('parts', 'holder'), 'query'), parts along dimension 0, may hold values from -0.5 to 0.5
Outputs:
- scores: float32 [32, 256], P(('parts', 'holder', 'query')), parts along dimension 0
The draws below stay inside these ranges and needn't reach their ends.
There are 2 independent parts, one for each index of `parts`. The reference program is written for one: setup_inputs(seed, part) draws one part's arguments, and reference() takes and returns one part's arrays. A program takes and returns all parts, laid end to end along the dimension named above; each array names one. Nothing has to cross between parts.
Inputs may be any that keep to these rules, and one draw needn't show every extreme that they name: `candidates`: each row names 256 different pages; no page is named by more than 16 rows, a bound that some block reaches. A permutation: page id p is stored at row page_slot[p] of page_embeddings.
All inputs are finite; a program needn't handle non-finite values.
Results may differ from the reference program's by a relative error of at most 0.0003.
Values may be sent and summed in bfloat16 or wider, within the bound.
A program may use at most 64 MiB of HBM per device.

```python
import math
import jax
import jax.numpy as jnp
import numpy as np
from jax import lax

E = 128
QT = 32
PATCH = 1024
K = 256
QUERIES = 16
PAGES = 512
CAP = 16


def steps_of(stream_key, extent, cuts, low, largest):
    loudness = 1.0
    for dim, parts in cuts:
        steps = jax.random.uniform(jax.random.fold_in(jax.random.fold_in(stream_key, 6), dim), (parts,), jnp.float32, low / len(cuts), largest / len(cuts))
        loudness = loudness * jnp.repeat(jnp.exp(steps), extent[dim] // parts).reshape((-1,) + (1,) * (len(extent) - 1 - dim))
    return loudness


def routed_block(rng, own, number, rows, count, top, reach, skew):
    ranking = jax.random.permutation(rng, count)
    crowded, ordinary = load_shares(count, rows * top, reach, skew, True), load_shares(count, rows * top, reach, skew, False)
    places = jnp.arange(count)

    def named(sizes, offset_by):
        used = int((sizes > 0).sum())
        fixed = max(1, used // 4)
        shifted = fixed + (places - fixed + offset_by * (used - fixed)) % max(1, count - fixed)
        return jnp.zeros((count,), jnp.int32).at[ranking[jnp.where(places < fixed, places, shifted)]].set(jnp.asarray(sizes, jnp.int32))

    sizes = jnp.where(number % 4 == 0, named(crowded, number // 4), named(ordinary, number - number // 4 - 1))
    mixed = jax.random.permutation(jax.random.fold_in(own, 3), count)
    source_of, sink = mixed[0:count // 2 * 2:2], mixed[1:count // 2 * 2:2]
    room = jnp.minimum(sizes[source_of] - 1, reach - sizes[sink]) // 2
    room = jnp.where((source_of == ranking[0]) | (sink == ranking[0]) | (sizes[sink] == 0), 0, jnp.maximum(room, 0))
    shifted = jax.random.randint(jax.random.fold_in(own, 4), (count // 2,), 0, 1 << 20) % (room + 1)
    sizes = sizes.at[source_of].add(-shifted).at[sink].add(shifted)
    members = jnp.searchsorted(jnp.cumsum(sizes), jnp.arange(rows * top), side="right").astype(jnp.int32)
    listing = members.reshape(top, rows).T
    listing = listing[jax.random.permutation(jax.random.fold_in(own, 1), rows)]
    offset_by = jax.random.randint(jax.random.fold_in(own, 2), (rows, 1), 0, top)
    return jnp.take_along_axis(listing, (jnp.arange(top)[None, :] + offset_by) % top, axis=1)


def load_shares(number_of, total, most, skew, full):
    portions = [(1 << 20) // math.isqrt(grade ** skew) + 1 for grade in range(1, number_of + 1)]
    largest = most if full else min(most, max(-(-total // number_of), total * portions[0] // sum(portions)))
    least = 1 if total - largest >= number_of - 1 else 0
    given, rest = [largest] + [least] * (number_of - 1), total - largest - least * (number_of - 1)
    while rest > 0:
        free = [i for i in range(1, number_of) if given[i] < largest] or [i for i in range(1, number_of) if given[i] < most]
        pool, left = sum([portions[i] for i in free]), rest
        for i in free:
            addition = min(most - given[i], max(1, left * portions[i] // pool), rest)
            given[i] = given[i] + addition
            rest = rest - addition
    return np.array(given)


def scatter_about(own_key, shape, scale, most, shards=(), kind=jnp.bfloat16):
    drawn = jax.random.normal(own_key, shape, jnp.float32) * scale
    if len(shards) > 0:
        drawn = steps_of(own_key, shape, shards, -0.22, 0.18) * drawn
    return jnp.clip(drawn, min=-most, max=most).astype(kind)


def setup_inputs(seed: int = 0, part: int = 0) -> dict:
    splits = jax.random.split(jax.random.key(seed), 5)
    part_keys = jax.random.split(jax.random.fold_in(splits[4], part), 5)
    queries = scatter_about(part_keys[0], (QUERIES, QT, E), 1.0, 6.0, ((0, 16),))
    candidates_keys = jax.random.split(jax.random.fold_in(part_keys[1], 1), QUERIES // QUERIES)
    candidates_turns = jax.random.permutation(jax.random.fold_in(part_keys[1], 3), QUERIES // QUERIES)
    candidates = jax.vmap(lambda own, number: routed_block(jax.random.fold_in(part_keys[1], 2), own, number, QUERIES, PAGES, K, CAP, 1))(candidates_keys, candidates_turns).reshape((QUERIES, K))
    page_slot = jax.random.permutation(part_keys[2], PAGES).astype(jnp.int32)
    page_embeddings = scatter_about(part_keys[3], (PAGES, PATCH, E), E ** -0.5, 0.5, ((0, 4), (1, 4)))
    return {"queries": queries, "candidates": candidates, "page_slot": page_slot, "page_embeddings": page_embeddings}


def reference(queries, candidates, page_slot, page_embeddings):
    def one_query(inputs):
        query_rows, wanted = inputs
        stored = jnp.take(page_slot, wanted, axis=0)
        chosen = jnp.take(page_embeddings, stored, axis=0)
        products = jnp.einsum("te,kpe->tkp", query_rows.astype(jnp.float32), chosen.astype(jnp.float32))
        best = jnp.max(products, axis=2)
        return jnp.sum(best, axis=0) / QT

    return lax.map(one_query, (queries, candidates))
```

```python
import functools

import jax
import jax.numpy as jnp
from jax import lax
from jax.experimental import pallas as pl
from jax.experimental.pallas import tpu as pltpu
from jax.sharding import PartitionSpec as P

MESH = pl.DeviceIdType.MESH
WIDE = 256
GROUP = 8
BLOCKS = 4
NT = (((1,), (1,)), ((), ()))
NN = (((1,), (0,)), ((), ()))


def split3(x):
    high = x.astype(jnp.bfloat16)
    rest = x - high.astype(jnp.float32)
    mid = rest.astype(jnp.bfloat16)
    low = (rest - mid.astype(jnp.float32)).astype(jnp.bfloat16)
    return high, mid, low


def dot(a, b, dims):
    return lax.dot_general(a, b, dims, preferred_element_type=jnp.float32)


def kernel(
    holders, askers, q_ref, cand_ref, slot_ref, emb_ref, out_ref,
    pages, qbuf, best, arrived, row, table,
    load_sem, qz_sem, qh_sem, qr_sem, ms_sem, mr_sem, ss_sem, sr_sem,
):
    h = lax.axis_index("holder")
    z = lax.axis_index("query")
    tokens = q_ref.shape[1]
    count, patches, width = pages.shape
    cols = holders * tokens
    block = count // BLOCKS
    z_peers = [lax.rem(z + d, askers) for d in range(1, askers)]
    h_peers = [lax.rem(h + d, holders) for d in range(1, holders)]

    loads = []
    for b in range(BLOCKS):
        part = pl.ds(b * block, block)
        load = pltpu.make_async_copy(emb_ref.at[part], pages.at[part], load_sem.at[b])
        load.start()
        loads.append(load)

    barrier = pltpu.get_barrier_semaphore()
    for peer in z_peers:
        pl.semaphore_signal(barrier, inc=1, device_id={"query": peer}, device_id_type=MESH)
    for peer in h_peers:
        pl.semaphore_signal(barrier, inc=1, device_id={"holder": peer}, device_id_type=MESH)

    slots = slot_ref[...]
    slot_rows = jnp.concatenate([slots // count, slots % count] + [jnp.zeros_like(slots)] * 6, axis=0)
    wanted = cand_ref[...]
    pages_in_all = slots.shape[1]
    ids = lax.broadcasted_iota(jnp.int32, (pages_in_all, wanted.shape[1]), 0)
    is_page = (ids == wanted).astype(jnp.float32).astype(jnp.bfloat16)
    place = dot(slot_rows.astype(jnp.float32).astype(jnp.bfloat16), is_page, NN)
    at_holder = place[0:1].astype(jnp.int32)
    at_row = place[1:2].astype(jnp.int32)
    row_ids = lax.broadcasted_iota(jnp.int32, (count, wanted.shape[1]), 0)
    is_row = (row_ids == at_row).astype(jnp.float32).astype(jnp.bfloat16)

    own = pl.ds(pl.multiple_of(h * tokens, tokens), tokens)
    qbuf[z, own, :] = q_ref[0]
    pl.semaphore_wait(barrier, askers + holders - 2)

    sends = []
    for peer in z_peers:
        copy = pltpu.make_async_remote_copy(
            src_ref=q_ref.at[0], dst_ref=qbuf.at[z, own], send_sem=qz_sem.at[peer],
            recv_sem=qr_sem.at[z, h], device_id={"query": peer}, device_id_type=MESH,
        )
        copy.start()
        sends.append(copy)

    def forward(at, src):
        for peer in h_peers:
            copy = pltpu.make_async_remote_copy(
                src_ref=src, dst_ref=qbuf.at[at, own], send_sem=qh_sem.at[at, peer],
                recv_sem=qr_sem.at[at, h], device_id={"holder": peer}, device_id_type=MESH,
            )
            copy.start()
            sends.append(copy)

    def await_query(at, who):
        rows = pl.ds(pl.multiple_of(who * tokens, tokens), tokens)
        pltpu.make_async_copy(qbuf.at[at, rows], qbuf.at[at, rows], qr_sem.at[at, who]).wait()

    forward(z, q_ref.at[0])
    for peer in z_peers:
        await_query(peer, h)
        forward(peer, qbuf.at[peer, own])

    together = max(1, WIDE // cols)
    if askers % together:
        together = 1
    rounds = askers // together
    mine = z // together
    for i in range(rounds):
        chunk = lax.rem(mine + 1 + i, rounds)
        first = chunk * together
        if i == rounds - 1:
            members = [first + lax.rem(lax.rem(z, together) + j, together) for j in range(together)]
            others = members[1:]
        else:
            members = [first + j for j in range(together)]
            others = members
        for at in members:
            for peer in h_peers:
                await_query(at, peer)
        for b in range(BLOCKS):
            if i == 0:
                loads[b].wait()

            def step(g, carry):
                start = pl.multiple_of(b * block + g * GROUP, GROUP)
                tall = pages[pl.ds(start, GROUP)].reshape(GROUP * patches, width)
                tok = qbuf[pl.ds(first, together)].reshape(together * cols, width)
                sims = dot(tall, tok, NT).reshape(GROUP, patches, together * cols)
                top = jnp.max(sims, axis=1)
                for j in range(together):
                    best[first + j, pl.ds(start, GROUP), :] = top[:, j * cols : (j + 1) * cols]
                return carry

            lax.fori_loop(0, block // GROUP, step, 0)
            part = pl.ds(b * block, block)
            for at in others:
                copy = pltpu.make_async_remote_copy(
                    src_ref=best.at[at, part], dst_ref=arrived.at[z, part], send_sem=ms_sem.at[at, b],
                    recv_sem=mr_sem.at[z, b], device_id={"query": at}, device_id_type=MESH,
                )
                copy.start()
                sends.append(copy)

    parts = []
    for b in range(BLOCKS):
        part = pl.ds(b * block, block)
        top = best[z, part, :]
        for peer in z_peers:
            pltpu.make_async_copy(arrived.at[peer, part], arrived.at[peer, part], mr_sem.at[peer, b]).wait()
            top = jnp.maximum(top, arrived[peer, part, :])
        parts.append(top)
    top = jnp.concatenate(parts, axis=0)
    tall = -(-holders // 8) * 8
    owner = lax.broadcasted_iota(jnp.int32, (tall, cols), 0)
    column = lax.broadcasted_iota(jnp.int32, (tall, cols), 1)
    low = owner * tokens
    member = ((column >= low) & (column < low + tokens)).astype(jnp.float32).astype(jnp.bfloat16)
    high, mid, rest = split3(top)
    scores = (dot(member, high, NT) + dot(member, mid, NT) + dot(member, rest, NT)) * (1.0 / tokens)
    for k in range(holders):
        row[k] = scores[k : k + 1]
    for peer in h_peers:
        copy = pltpu.make_async_remote_copy(
            src_ref=row.at[peer], dst_ref=table.at[h], send_sem=ss_sem.at[peer],
            recv_sem=sr_sem.at[h], device_id={"holder": peer}, device_id_type=MESH,
        )
        copy.start()
        sends.append(copy)
    table[h] = row[h]
    for peer in h_peers:
        pltpu.make_async_copy(table.at[peer], table.at[peer], sr_sem.at[peer]).wait()

    known = [table[k] for k in range(holders)]
    known = jnp.concatenate(known + [jnp.zeros_like(known[0])] * (tall - holders), axis=0)
    high, mid, rest = split3(known)
    found = dot(high, is_row, NN) + dot(mid, is_row, NN) + dot(rest, is_row, NN)
    holder_ids = lax.broadcasted_iota(jnp.int32, found.shape, 0)
    out_ref[...] = jnp.sum(jnp.where(holder_ids == at_holder, found, 0.0), axis=0, keepdims=True)
    for copy in sends:
        copy.wait_send()


def shards(holders, askers, queries, candidates, page_slot, page_embeddings):
    _, tokens, width = queries.shape
    count, patches, _ = page_embeddings.shape
    cols = holders * tokens
    vmem = pl.BlockSpec(memory_space=pltpu.VMEM)
    dma = pltpu.SemaphoreType.DMA
    return pl.pallas_call(
        functools.partial(kernel, holders, askers),
        out_shape=jax.ShapeDtypeStruct(candidates.shape, jnp.float32),
        in_specs=[vmem, vmem, vmem, pl.BlockSpec(memory_space=pl.ANY)],
        out_specs=vmem,
        scratch_shapes=[
            pltpu.VMEM((count, patches, width), jnp.bfloat16),
            pltpu.VMEM((askers, cols, width), jnp.bfloat16),
            pltpu.VMEM((askers, count, cols), jnp.float32),
            pltpu.VMEM((askers, count, cols), jnp.float32),
            pltpu.VMEM((holders, 1, count), jnp.float32),
            pltpu.VMEM((holders, 1, count), jnp.float32),
            dma((BLOCKS,)),
            dma((askers,)),
            dma((askers, holders)),
            dma((askers, holders)),
            dma((askers, BLOCKS)),
            dma((askers, BLOCKS)),
            dma((holders,)),
            dma((holders,)),
        ],
        compiler_params=pltpu.CompilerParams(
            collective_id=0, has_side_effects=True, vmem_limit_bytes=48 * 1024 * 1024
        ),
    )(queries, candidates, page_slot.reshape(1, -1), page_embeddings)


def solution(mesh):
    placed = (
        P(("parts", "holder", "query"), None, None),
        P(("parts", "holder", "query"), None),
        P("parts"),
        P(("parts", "holder"), "query", None),
    )
    return jax.shard_map(
        functools.partial(shards, mesh.shape["holder"], mesh.shape["query"]),
        mesh=mesh,
        in_specs=placed,
        out_specs=P(("parts", "holder", "query"), None),
        check_vma=False,
    )
```

```python
import functools

import jax
import jax.numpy as jnp
from jax import lax
from jax.experimental import pallas as pl
from jax.experimental.pallas import tpu as pltpu
from jax.sharding import PartitionSpec as P

MESH = pl.DeviceIdType.MESH
WIDE = 256
BLOCKS = 4
NT = (((1,), (1,)), ((), ()))
NN = (((1,), (0,)), ((), ()))


def split3(x):
    high = x.astype(jnp.bfloat16)
    rest = x - high.astype(jnp.float32)
    mid = rest.astype(jnp.bfloat16)
    low = (rest - mid.astype(jnp.float32)).astype(jnp.bfloat16)
    return high, mid, low


def dot(a, b, dims):
    return lax.dot_general(a, b, dims, preferred_element_type=jnp.float32)


def kernel(
    holders, askers, q_ref, cand_ref, slot_ref, emb_ref, out_ref,
    pages, qbuf, best, arrived, row, table, cand, slot,
    load_sem, own_sem, in_sem, qz_sem, qh_sem, qr_sem, ms_sem, mr_sem, ss_sem, sr_sem,
):
    h = lax.axis_index("holder")
    z = lax.axis_index("query")
    tokens = q_ref.shape[1]
    count, patches, width = pages.shape
    cols = holders * tokens
    block = count // BLOCKS
    z_peers = [lax.rem(z + d, askers) for d in range(1, askers)]
    h_peers = [lax.rem(h + d, holders) for d in range(1, holders)]

    own = pl.ds(pl.multiple_of(h * tokens, tokens), tokens)
    keep = pltpu.make_async_copy(q_ref.at[0], qbuf.at[z, own], own_sem)
    keep.start()
    small = [
        pltpu.make_async_copy(slot_ref, slot, in_sem.at[0]),
        pltpu.make_async_copy(cand_ref, cand, in_sem.at[1]),
    ]
    for copy in small:
        copy.start()

    def block_of(b):
        return pl.ds(pl.multiple_of(b * block, block), block)

    def load(b):
        return pltpu.make_async_copy(emb_ref.at[block_of(b)], pages.at[block_of(b)], load_sem.at[b])

    for b in range(BLOCKS):
        load(b).start()

    barrier = pltpu.get_barrier_semaphore()
    for peer in z_peers:
        pl.semaphore_signal(barrier, inc=1, device_id={"query": peer}, device_id_type=MESH)
    for peer in h_peers:
        pl.semaphore_signal(barrier, inc=1, device_id={"holder": peer}, device_id_type=MESH)

    pl.semaphore_wait(barrier, askers + holders - 2)

    sends = []
    for peer in z_peers:
        copy = pltpu.make_async_remote_copy(
            src_ref=q_ref.at[0], dst_ref=qbuf.at[z, own], send_sem=qz_sem.at[peer],
            recv_sem=qr_sem.at[z, h], device_id={"query": peer}, device_id_type=MESH,
        )
        copy.start()
        sends.append(copy)

    def forward(at, src):
        for peer in h_peers:
            copy = pltpu.make_async_remote_copy(
                src_ref=src, dst_ref=qbuf.at[at, own], send_sem=qh_sem.at[at, peer],
                recv_sem=qr_sem.at[at, h], device_id={"holder": peer}, device_id_type=MESH,
            )
            copy.start()
            sends.append(copy)

    def await_query(at, who):
        rows = pl.ds(pl.multiple_of(who * tokens, tokens), tokens)
        pltpu.make_async_copy(qbuf.at[at, rows], qbuf.at[at, rows], qr_sem.at[at, who]).wait()

    forward(z, q_ref.at[0])

    for copy in small:
        copy.wait()
    slots = slot[...]
    slot_rows = jnp.concatenate([slots // count, slots % count] + [jnp.zeros_like(slots)] * 6, axis=0)
    wanted = cand[...]
    pages_in_all = slots.shape[1]
    ids = lax.broadcasted_iota(jnp.int32, (pages_in_all, wanted.shape[1]), 0)
    is_page = (ids == wanted).astype(jnp.float32).astype(jnp.bfloat16)
    place = dot(slot_rows.astype(jnp.float32).astype(jnp.bfloat16), is_page, NN)
    at_holder = place[0:1].astype(jnp.int32)
    at_row = place[1:2].astype(jnp.int32)
    row_ids = lax.broadcasted_iota(jnp.int32, (count, wanted.shape[1]), 0)
    is_row = (row_ids == at_row).astype(jnp.float32).astype(jnp.bfloat16)

    keep.wait()
    for peer in z_peers:
        await_query(peer, h)
        forward(peer, qbuf.at[peer, own])

    together = max(1, WIDE // cols)
    if askers % together:
        together = 1
    rounds = askers // together

    def hand_over(at, b):
        return pltpu.make_async_remote_copy(
            src_ref=best.at[at, block_of(b)], dst_ref=arrived.at[z, block_of(b)], send_sem=ms_sem.at[at, b],
            recv_sem=mr_sem.at[z, b], device_id={"query": at}, device_id_type=MESH,
        )

    mine = z // together
    for i in range(rounds):
        chunk = lax.rem(mine + 1 + i, rounds)
        first = chunk * together
        if i == rounds - 1:
            members = [first + lax.rem(lax.rem(z, together) + j, together) for j in range(together)]
            others = members[1:]
        else:
            members = [first + j for j in range(together)]
            others = members
        for at in members:
            for peer in h_peers:
                await_query(at, peer)

        def work(b, carry):
            if i == 0:
                load(b).wait()
            part = block_of(b)
            tall = pages[part].reshape(block * patches, width)
            tok = qbuf[pl.ds(first, together)].reshape(together * cols, width)
            sims = dot(tall, tok, NT).reshape(block, patches, together * cols)
            top = jnp.max(sims, axis=1)
            for j in range(together):
                best[first + j, part, :] = top[:, j * cols : (j + 1) * cols]
            for at in others:
                hand_over(at, b).start()
            return carry

        lax.fori_loop(0, BLOCKS, work, 0)

    parts = []
    for b in range(BLOCKS):
        part = pl.ds(b * block, block)
        top = best[z, part, :]
        for peer in z_peers:
            pltpu.make_async_copy(arrived.at[peer, part], arrived.at[peer, part], mr_sem.at[peer, b]).wait()
            top = jnp.maximum(top, arrived[peer, part, :])
        parts.append(top)
    top = jnp.concatenate(parts, axis=0)
    tall = -(-holders // 8) * 8
    owner = lax.broadcasted_iota(jnp.int32, (tall, cols), 0)
    column = lax.broadcasted_iota(jnp.int32, (tall, cols), 1)
    low = owner * tokens
    member = ((column >= low) & (column < low + tokens)).astype(jnp.float32).astype(jnp.bfloat16)
    high, mid, rest = split3(top)
    scores = (dot(member, high, NT) + dot(member, mid, NT) + dot(member, rest, NT)) * (1.0 / tokens)
    for k in range(holders):
        row[k] = scores[k : k + 1]
    for peer in h_peers:
        copy = pltpu.make_async_remote_copy(
            src_ref=row.at[peer], dst_ref=table.at[h], send_sem=ss_sem.at[peer],
            recv_sem=sr_sem.at[h], device_id={"holder": peer}, device_id_type=MESH,
        )
        copy.start()
        sends.append(copy)
    table[h] = row[h]
    for peer in h_peers:
        pltpu.make_async_copy(table.at[peer], table.at[peer], sr_sem.at[peer]).wait()

    known = [table[k] for k in range(holders)]
    known = jnp.concatenate(known + [jnp.zeros_like(known[0])] * (tall - holders), axis=0)
    high, mid, rest = split3(known)
    found = dot(high, is_row, NN) + dot(mid, is_row, NN) + dot(rest, is_row, NN)
    holder_ids = lax.broadcasted_iota(jnp.int32, found.shape, 0)
    out_ref[...] = jnp.sum(jnp.where(holder_ids == at_holder, found, 0.0), axis=0, keepdims=True)
    for copy in sends:
        copy.wait_send()
    for peer in z_peers:
        for b in range(BLOCKS):
            hand_over(peer, b).wait_send()


def shards(holders, askers, queries, candidates, page_slot, page_embeddings):
    _, tokens, width = queries.shape
    count, patches, _ = page_embeddings.shape
    cols = holders * tokens
    vmem = pl.BlockSpec(memory_space=pltpu.VMEM)
    dma = pltpu.SemaphoreType.DMA
    return pl.pallas_call(
        functools.partial(kernel, holders, askers),
        out_shape=jax.ShapeDtypeStruct(candidates.shape, jnp.float32),
        in_specs=[pl.BlockSpec(memory_space=pl.ANY)] * 4,
        out_specs=vmem,
        scratch_shapes=[
            pltpu.VMEM((count, patches, width), jnp.bfloat16),
            pltpu.VMEM((askers, cols, width), jnp.bfloat16),
            pltpu.VMEM((askers, count, cols), jnp.float32),
            pltpu.VMEM((askers, count, cols), jnp.float32),
            pltpu.VMEM((holders, 1, count), jnp.float32),
            pltpu.VMEM((holders, 1, count), jnp.float32),
            pltpu.VMEM(candidates.shape, jnp.int32),
            pltpu.VMEM((1, page_slot.shape[0]), jnp.int32),
            dma((BLOCKS,)),
            dma,
            dma((2,)),
            dma((askers,)),
            dma((askers, holders)),
            dma((askers, holders)),
            dma((askers, BLOCKS)),
            dma((askers, BLOCKS)),
            dma((holders,)),
            dma((holders,)),
        ],
        compiler_params=pltpu.CompilerParams(
            collective_id=0, has_side_effects=True, vmem_limit_bytes=64 * 1024 * 1024
        ),
    )(queries, candidates, page_slot.reshape(1, -1), page_embeddings)


def solution(mesh):
    placed = (
        P(("parts", "holder", "query"), None, None),
        P(("parts", "holder", "query"), None),
        P("parts"),
        P(("parts", "holder"), "query", None),
    )
    return jax.shard_map(
        functools.partial(shards, mesh.shape["holder"], mesh.shape["query"]),
        mesh=mesh,
        in_specs=placed,
        out_specs=P(("parts", "holder", "query"), None),
        check_vma=False,
    )
```

```python
import functools

import jax
import jax.numpy as jnp
from jax import lax
from jax.experimental import pallas as pl
from jax.experimental.pallas import tpu as pltpu
from jax.sharding import PartitionSpec as P

MESH = pl.DeviceIdType.MESH
WIDE = 256
BLOCKS = 4
NT = (((1,), (1,)), ((), ()))
NN = (((1,), (0,)), ((), ()))


def split3(x):
    high = x.astype(jnp.bfloat16)
    rest = x - high.astype(jnp.float32)
    mid = rest.astype(jnp.bfloat16)
    low = (rest - mid.astype(jnp.float32)).astype(jnp.bfloat16)
    return high, mid, low


def dot(a, b, dims):
    return lax.dot_general(a, b, dims, preferred_element_type=jnp.float32)


def kernel(
    holders, askers, q_ref, cand_ref, slot_ref, emb_ref, out_ref,
    pages, qbuf, best, arrived, row, table, cand, slot,
    load_sem, own_sem, in_sem, qh_sem, qr_sem, ms_sem, mr_sem, ss_sem, sr_sem,
):
    h = lax.axis_index("holder")
    z = lax.axis_index("query")
    tokens = q_ref.shape[1]
    count, patches, width = pages.shape
    cols = holders * tokens
    block = count // BLOCKS
    z_peers = [lax.rem(z + d, askers) for d in range(1, askers)]
    h_peers = [lax.rem(h + d, holders) for d in range(1, holders)]
    middle = askers // 2
    far = [(dz, dh) for dz in range(askers) for dh in range(holders) if dz or dh]
    far.sort(key=lambda d: abs(abs(d[0] - middle) - middle))

    own = pl.ds(pl.multiple_of(h * tokens, tokens), tokens)
    keep = pltpu.make_async_copy(q_ref.at[0], qbuf.at[z, own], own_sem)
    keep.start()
    small = [
        pltpu.make_async_copy(slot_ref, slot, in_sem.at[0]),
        pltpu.make_async_copy(cand_ref, cand, in_sem.at[1]),
    ]
    for copy in small:
        copy.start()

    def block_of(b):
        return pl.ds(pl.multiple_of(b * block, block), block)

    def load(b):
        return pltpu.make_async_copy(emb_ref.at[block_of(b)], pages.at[block_of(b)], load_sem.at[b])

    load(0).start()

    barrier = pltpu.get_barrier_semaphore()
    for dz, dh in far:
        at, peer = lax.rem(z + dz, askers), lax.rem(h + dh, holders)
        pl.semaphore_signal(barrier, inc=1, device_id={"holder": peer, "query": at}, device_id_type=MESH)
    pl.semaphore_wait(barrier, askers * holders - 1)

    sends = []
    for dz, dh in far:
        at, peer = lax.rem(z + dz, askers), lax.rem(h + dh, holders)
        copy = pltpu.make_async_remote_copy(
            src_ref=q_ref.at[0], dst_ref=qbuf.at[z, own], send_sem=qh_sem.at[at, peer],
            recv_sem=qr_sem.at[z, h], device_id={"holder": peer, "query": at}, device_id_type=MESH,
        )
        copy.start()
        sends.append(copy)

    for b in range(1, BLOCKS):
        load(b).start()

    def await_query(at, who):
        rows = pl.ds(pl.multiple_of(who * tokens, tokens), tokens)
        pltpu.make_async_copy(qbuf.at[at, rows], qbuf.at[at, rows], qr_sem.at[at, who]).wait()

    keep.wait()

    together = max(1, WIDE // cols)
    if askers % together:
        together = 1
    rounds = askers // together

    def hand_over(at, b):
        return pltpu.make_async_remote_copy(
            src_ref=best.at[at, block_of(b)], dst_ref=arrived.at[z, block_of(b)], send_sem=ms_sem.at[at, b],
            recv_sem=mr_sem.at[z, b], device_id={"query": at}, device_id_type=MESH,
        )

    mine = z // together
    early = BLOCKS // 2
    order = [(0, 0, early)] + [(i, 0, BLOCKS) for i in range(1, rounds)] + [(0, early, BLOCKS)]
    for turn, (i, begin, end) in enumerate(order):
        first = lax.rem(mine + i, rounds) * together
        if i == 0:
            members = [first + lax.rem(lax.rem(z, together) + j, together) for j in range(together)]
            others = members[1:]
        else:
            members = [first + j for j in range(together)]
            others = members
        if turn == 1:
            for b in range(early, BLOCKS):
                load(b).wait()
        if begin == 0:
            for at in members:
                for peer in h_peers:
                    await_query(at, peer)
            for at in others:
                await_query(at, h)

        def work(b, carry):
            if turn == 0:
                load(b).wait()
            part = block_of(b)
            tall = pages[part].reshape(block * patches, width)
            tok = qbuf[pl.ds(first, together)].reshape(together * cols, width)
            sims = dot(tall, tok, NT).reshape(block, patches, together * cols)
            top = jnp.max(sims, axis=1)
            for j in range(together):
                best[first + j, part, :] = top[:, j * cols : (j + 1) * cols]
            for at in others:
                hand_over(at, b).start()
            return carry

        lax.fori_loop(begin, end, work, 0)

    for copy in small:
        copy.wait()
    slots = slot[...]
    slot_rows = jnp.concatenate([slots // count, slots % count] + [jnp.zeros_like(slots)] * 6, axis=0)
    wanted = cand[...]
    pages_in_all = slots.shape[1]
    ids = lax.broadcasted_iota(jnp.int32, (pages_in_all, wanted.shape[1]), 0)
    is_page = (ids == wanted).astype(jnp.float32).astype(jnp.bfloat16)
    place = dot(slot_rows.astype(jnp.float32).astype(jnp.bfloat16), is_page, NN)
    at_holder = place[0:1].astype(jnp.int32)
    at_row = place[1:2].astype(jnp.int32)
    row_ids = lax.broadcasted_iota(jnp.int32, (count, wanted.shape[1]), 0)
    is_row = (row_ids == at_row).astype(jnp.float32).astype(jnp.bfloat16)

    parts = []
    for b in range(BLOCKS):
        part = pl.ds(b * block, block)
        top = best[z, part, :]
        for peer in z_peers:
            pltpu.make_async_copy(arrived.at[peer, part], arrived.at[peer, part], mr_sem.at[peer, b]).wait()
            top = jnp.maximum(top, arrived[peer, part, :])
        parts.append(top)
    top = jnp.concatenate(parts, axis=0)
    tall = -(-holders // 8) * 8
    owner = lax.broadcasted_iota(jnp.int32, (tall, cols), 0)
    column = lax.broadcasted_iota(jnp.int32, (tall, cols), 1)
    low = owner * tokens
    member = ((column >= low) & (column < low + tokens)).astype(jnp.float32).astype(jnp.bfloat16)
    high, mid, rest = split3(top)
    scores = (dot(member, high, NT) + dot(member, mid, NT) + dot(member, rest, NT)) * (1.0 / tokens)
    for k in range(holders):
        row[k] = scores[k : k + 1]
    for peer in h_peers:
        copy = pltpu.make_async_remote_copy(
            src_ref=row.at[peer], dst_ref=table.at[h], send_sem=ss_sem.at[peer],
            recv_sem=sr_sem.at[h], device_id={"holder": peer}, device_id_type=MESH,
        )
        copy.start()
        sends.append(copy)
    table[h] = row[h]
    for peer in h_peers:
        pltpu.make_async_copy(table.at[peer], table.at[peer], sr_sem.at[peer]).wait()

    known = [table[k] for k in range(holders)]
    known = jnp.concatenate(known + [jnp.zeros_like(known[0])] * (tall - holders), axis=0)
    high, mid, rest = split3(known)
    found = dot(high, is_row, NN) + dot(mid, is_row, NN) + dot(rest, is_row, NN)
    holder_ids = lax.broadcasted_iota(jnp.int32, found.shape, 0)
    out_ref[...] = jnp.sum(jnp.where(holder_ids == at_holder, found, 0.0), axis=0, keepdims=True)
    for copy in sends:
        copy.wait_send()
    for peer in z_peers:
        for b in range(BLOCKS):
            hand_over(peer, b).wait_send()


def shards(holders, askers, queries, candidates, page_slot, page_embeddings):
    _, tokens, width = queries.shape
    count, patches, _ = page_embeddings.shape
    cols = holders * tokens
    vmem = pl.BlockSpec(memory_space=pltpu.VMEM)
    dma = pltpu.SemaphoreType.DMA
    return pl.pallas_call(
        functools.partial(kernel, holders, askers),
        out_shape=jax.ShapeDtypeStruct(candidates.shape, jnp.float32),
        in_specs=[pl.BlockSpec(memory_space=pl.ANY)] * 4,
        out_specs=vmem,
        scratch_shapes=[
            pltpu.VMEM((count, patches, width), jnp.bfloat16),
            pltpu.VMEM((askers, cols, width), jnp.bfloat16),
            pltpu.VMEM((askers, count, cols), jnp.float32),
            pltpu.VMEM((askers, count, cols), jnp.float32),
            pltpu.VMEM((holders, 1, count), jnp.float32),
            pltpu.VMEM((holders, 1, count), jnp.float32),
            pltpu.VMEM(candidates.shape, jnp.int32),
            pltpu.VMEM((1, page_slot.shape[0]), jnp.int32),
            dma((BLOCKS,)),
            dma,
            dma((2,)),
            dma((askers, holders)),
            dma((askers, holders)),
            dma((askers, BLOCKS)),
            dma((askers, BLOCKS)),
            dma((holders,)),
            dma((holders,)),
        ],
        compiler_params=pltpu.CompilerParams(
            collective_id=0, has_side_effects=True, vmem_limit_bytes=64 * 1024 * 1024
        ),
    )(queries, candidates, page_slot.reshape(1, -1), page_embeddings)


def solution(mesh):
    placed = (
        P(("parts", "holder", "query"), None, None),
        P(("parts", "holder", "query"), None),
        P("parts"),
        P(("parts", "holder"), "query", None),
    )
    return jax.shard_map(
        functools.partial(shards, mesh.shape["holder"], mesh.shape["query"]),
        mesh=mesh,
        in_specs=placed,
        out_specs=P(("parts", "holder", "query"), None),
        check_vma=False,
    )
```
